32 devices in a mesh: ctx: 8 (over z, x), tp: 4 (over y, core).
Axes of the slice: x: 2, y: 2, z: 4, core: 2. Of those that a mesh axis runs over, the one named last changes fastest.
Arguments:
- hidden_in: bfloat16 [2048, 3072], P('ctx', 'tp'), may hold values from -96 to 96
- norm_gain: float32 [3072], replicated, may hold values from 0.1 to 1.9
- w_query: bfloat16 [3072, 3072], P(None, 'tp'), may hold values from -1 to 1
- w_key: bfloat16 [3072, 3072], P(None, 'tp'), may hold values from -1 to 1
- w_value: bfloat16 [3072, 3072], P(None, 'tp'), may hold values from -0.109375 to 0.109375
- w_out: bfloat16 [3072, 3072], P('tp'), may hold values from -0.109375 to 0.109375
- head_gain: float32 [3072], replicated, may hold values from 0.1 to 1.9
- proj_head: bfloat16 [3072, 2048], P('tp'), may hold values from -0.109375 to 0.109375
- proj_middle: bfloat16 [3072, 512], P('tp'), may hold values from -0.109375 to 0.109375
- proj_tail: bfloat16 [3072, 128], P('tp'), may hold values from -0.109375 to 0.109375
- table_head: bfloat16 [10240, 2048], P(('tp', 'ctx')), may hold values from -64 to 64
- table_middle: bfloat16 [20480, 512], P(('tp', 'ctx')), may hold values from -64 to 64
- table_tail: bfloat16 [104448, 128], P(('tp', 'ctx')), may hold values from -64 to 64
- clusters: bfloat16 [2, 2048], replicated, may hold values from -0.375 to 0.375
- targets: int32 [2048], P('ctx'), may hold values from 0 to 135167
Outputs:
- hidden_out: bfloat16 [2048, 3072], P('ctx', 'tp')
- losses: float32 [2048], P('ctx')
The draws below stay inside these ranges and needn't reach their ends.
All inputs are finite; a program needn't handle non-finite values.
Results may differ from the reference program's by a relative error of at most 0.004.
Values may be sent and summed in bfloat16 or wider, within the bound.
A program may use at most 128 MiB of HBM per device.

```python
import math
import jax
import jax.numpy as jnp
import numpy as np
from jax import lax

D = 3072
HEADS = 32
HD = 96
P0 = 2048
P1 = 512
P2 = 128
V0 = 10240
V1 = 20480
V2 = 104448
SEG = 256
VOCAB = 135168
TOKENS = 2048
N_CTX = 8
N_TP = 4


def draw_hidden_in(key, part):
    base_key = jax.random.fold_in(key, 6101)
    feature_pos = jnp.arange(D, dtype=jnp.float32) / (D - 1)
    rough = jnp.exp(jax.random.uniform(jax.random.fold_in(base_key, 1), (D,), jnp.float32, math.log(0.7), math.log(1.4)))
    entries = jnp.clip(jax.random.normal(jax.random.fold_in(base_key, 2), (TOKENS, D), jnp.float32), -6.0, 6.0)
    ramp = jnp.exp(feature_pos * math.log(6.0)) * rough
    values = entries * ramp[None, :]
    return jnp.clip(values, -96.0, 96.0).astype(jnp.bfloat16)


def attention_pair(key):
    base_key = jax.random.fold_in(key, 7101)
    query_part = jax.random.normal(jax.random.fold_in(base_key, 1), (D, HEADS * HD), jnp.float32) * D ** (-0.5)
    key_part = jax.random.normal(jax.random.fold_in(base_key, 2), (D, HEADS * HD), jnp.float32) * D ** (-0.5)
    return (jnp.clip(query_part, -1.0, 1.0), jnp.clip(key_part, -1.0, 1.0))


def draw_w_query(key, part):
    return attention_pair(key)[0].astype(jnp.bfloat16)


def draw_w_key(key, part):
    return attention_pair(key)[1].astype(jnp.bfloat16)


def band_table(key, salt, row_total, table_width):
    table_key = jax.random.fold_in(key, salt)
    entries = jax.random.normal(jax.random.fold_in(table_key, 1), (row_total, table_width), jnp.float32) * (3.0 / math.sqrt(table_width))
    return jnp.clip(entries, -64.0, 64.0).astype(jnp.bfloat16)


def draw_table_head(key, part):
    return band_table(key, 8101, V0, P0)


def draw_table_middle(key, part):
    return band_table(key, 8102, V1, P1)


def draw_table_tail(key, part):
    return band_table(key, 8103, V2, P2)


def place_ends(array, stream_key, least, high):
    extent = array.shape
    place = [jax.random.randint(jax.random.fold_in(stream_key, axis), (), 0, extent[axis]) for axis in range(len(extent))]
    array = array.at[tuple(place)].set(least)
    longest = extent.index(max(extent))
    place[longest] = (place[longest] + 1) % extent[longest]
    return array.at[tuple(place)].set(high)


def block_levels(key, extent, split, least, high):
    factor_of = 1.0
    for position, parts in split:
        heights = jax.random.uniform(jax.random.fold_in(jax.random.fold_in(key, 6), position), (parts,), jnp.float32, least / len(split), high / len(split))
        factor_of = factor_of * jnp.repeat(jnp.exp(heights), extent[position] // parts).reshape((-1,) + (1,) * (len(extent) - 1 - position))
    return factor_of


def skewed_wide(key, extent, number_of, slope):
    loads = [min(1 << octave, number_of + 1 - (1 << octave)) * (1 << 20) // math.isqrt((1 << octave) ** slope) + 1 for octave in range((number_of + 1).bit_length()) if 1 << octave <= number_of]
    deviation = 1 + sum(loads) // (1 << 30)
    table = np.cumsum(np.array([max(1, weight // deviation) for weight in loads]))
    pick = jax.random.randint(jax.random.fold_in(key, 1), extent, 0, int(table[len(loads) - 1]))
    start = jnp.left_shift(1, jnp.searchsorted(jnp.asarray(table, jnp.int32), pick, side="right").astype(jnp.int32))
    rank = start - 1 + jax.random.randint(jax.random.fold_in(key, 4), extent, 0, 1 << 30) % jnp.minimum(start, number_of + 1 - start)
    return jax.random.permutation(jax.random.fold_in(key, 2), number_of)[rank].astype(jnp.int32)


def normal_values(rng, shape, scale, limit, split=(), kind=jnp.bfloat16):
    values = jax.random.normal(rng, shape, jnp.float32) * scale
    if len(split) > 0:
        values = block_levels(rng, shape, split, -0.22, 0.18) * values
    return jnp.clip(values, min=-limit, max=limit).astype(kind)


def setup_inputs(seed: int = 0) -> dict:
    keys = jax.random.split(jax.random.key(seed), 16)
    hidden_in = draw_hidden_in(jax.random.fold_in(keys[15], 71), 0)
    norm_gain = jnp.clip(1.0 + 0.18 * jax.random.normal(keys[1], (D,), jnp.float32), 0.1, 1.9)
    w_query = draw_w_query(jax.random.fold_in(keys[15], 71), 0)
    w_key = draw_w_key(jax.random.fold_in(keys[15], 71), 0)
    w_value = normal_values(keys[4], (D, HEADS * HD), D ** -0.5, 0.109375, ((1, 4),))
    w_out = normal_values(keys[5], (HEADS * HD, D), (HEADS * HD) ** -0.5, 0.109375, ((0, 4),))
    head_gain = jnp.clip(1.0 + 0.18 * jax.random.normal(keys[6], (D,), jnp.float32), 0.1, 1.9)
    proj_head = normal_values(keys[7], (D, P0), D ** -0.5, 0.109375, ((0, 4),))
    proj_middle = normal_values(keys[8], (D, P1), D ** -0.5, 0.109375, ((0, 4),))
    proj_tail = normal_values(keys[9], (D, P2), D ** -0.5, 0.109375, ((0, 4),))
    table_head = draw_table_head(jax.random.fold_in(keys[15], 71), 0)
    table_middle = draw_table_middle(jax.random.fold_in(keys[15], 71), 0)
    table_tail = draw_table_tail(jax.random.fold_in(keys[15], 71), 0)
    clusters = normal_values(keys[13], (2, P0), (P0 // 9) ** -0.5, 0.375)
    targets = place_ends(skewed_wide(keys[14], (TOKENS,), VOCAB, 2), jax.random.fold_in(keys[14], 3), 0, VOCAB - 1).astype(jnp.int32)
    return {"hidden_in": hidden_in, "norm_gain": norm_gain, "w_query": w_query, "w_key": w_key, "w_value": w_value, "w_out": w_out, "head_gain": head_gain, "proj_head": proj_head, "proj_middle": proj_middle, "proj_tail": proj_tail, "table_head": table_head, "table_middle": table_middle, "table_tail": table_tail, "clusters": clusters, "targets": targets}


def norm_rows(row_values, gain_vector):
    mean_sq = lax.optimization_barrier(jnp.mean(row_values * row_values, axis=1, keepdims=True))
    return row_values * lax.rsqrt(mean_sq + 1e-06) * gain_vector

def grouped_product(left_side, right_side, group_count):
    group_width = left_side.shape[1] // group_count
    result = jnp.zeros((left_side.shape[0], right_side.shape[1]), jnp.float32)
    for group_idx in range(group_count):
        lower = group_idx * group_width
        partial_term = jnp.dot(left_side[:, lower:lower + group_width], right_side[lower:lower + group_width], preferred_element_type=jnp.float32)
        rounded = lax.optimization_barrier(partial_term.astype(jnp.bfloat16))
        result = result + rounded.astype(jnp.float32)
    return result

def reference(hidden_in, norm_gain, w_query, w_key, w_value, w_out, head_gain, proj_head, proj_middle, proj_tail, table_head, table_middle, table_tail, clusters, targets):
    width_all = HEADS * HD
    inputs32 = hidden_in.astype(jnp.float32)
    normed = norm_rows(inputs32, norm_gain).astype(jnp.bfloat16)
    queries = jnp.dot(normed, w_query, preferred_element_type=jnp.float32).astype(jnp.bfloat16)
    key_all = jnp.dot(normed, w_key, preferred_element_type=jnp.float32).astype(jnp.bfloat16)
    value_all = jnp.dot(normed, w_value, preferred_element_type=jnp.float32).astype(jnp.bfloat16)
    padded_keys = jnp.concatenate([jnp.zeros((SEG, width_all), jnp.bfloat16), key_all], 0)
    padded_values = jnp.concatenate([jnp.zeros((SEG, width_all), jnp.bfloat16), value_all], 0)

    def segment_context(segment):
        row_start = (segment * SEG).astype(jnp.int32)
        query_rows = lax.dynamic_slice_in_dim(queries, row_start, SEG, 0).reshape(SEG, HEADS, HD).astype(jnp.float32)
        key_rows = lax.dynamic_slice_in_dim(padded_keys, row_start, 2 * SEG, 0).reshape(2 * SEG, HEADS, HD).astype(jnp.float32)
        value_rows = lax.dynamic_slice_in_dim(padded_values, row_start, 2 * SEG, 0).reshape(2 * SEG, HEADS, HD).astype(jnp.float32)
        scores = jnp.einsum('qhe,khe->hqk', query_rows, key_rows) * HD ** (-0.5)
        row_pos = lax.broadcasted_iota(jnp.int32, (SEG, 2 * SEG), 0)
        col_pos = lax.broadcasted_iota(jnp.int32, (SEG, 2 * SEG), 1)
        allowed = jnp.where(col_pos < SEG, segment > 0, col_pos - SEG <= row_pos)
        scores = jnp.where(allowed[None], scores, -1e+30)
        top_score = lax.optimization_barrier(jnp.max(scores, axis=2, keepdims=True))
        raised = jnp.exp(scores - top_score)
        weights = (raised / lax.optimization_barrier(jnp.sum(raised, axis=2, keepdims=True))).astype(jnp.bfloat16)
        mixed_rows = jnp.einsum('hqk,khe->qhe', weights.astype(jnp.float32), value_rows)
        return mixed_rows.astype(jnp.bfloat16).reshape(SEG, width_all)
    segment_ids = jnp.arange(N_CTX, dtype=jnp.int32)
    context = lax.map(segment_context, segment_ids).reshape(SEG * N_CTX, width_all)
    attention = grouped_product(context, w_out, N_TP)
    summed = inputs32 + attention
    hidden_out = summed.astype(jnp.bfloat16)
    normed_out = norm_rows(summed, head_gain).astype(jnp.bfloat16)
    band_head = grouped_product(normed_out, proj_head, N_TP).astype(jnp.bfloat16)
    band_middle = grouped_product(normed_out, proj_middle, N_TP).astype(jnp.bfloat16)
    band_tail = grouped_product(normed_out, proj_tail, N_TP).astype(jnp.bfloat16)

    def segment_loss(segment):
        row_start = (segment * SEG).astype(jnp.int32)
        head_rows = lax.dynamic_slice_in_dim(band_head, row_start, SEG, 0)
        middle_rows = lax.dynamic_slice_in_dim(band_middle, row_start, SEG, 0)
        tail_rows = lax.dynamic_slice_in_dim(band_tail, row_start, SEG, 0)
        goal = lax.dynamic_slice_in_dim(targets, row_start, SEG, 0)
        words = jnp.dot(head_rows, table_head.T, preferred_element_type=jnp.float32)
        cluster_logits = jnp.dot(head_rows, clusters.T, preferred_element_type=jnp.float32)
        head_total = jax.nn.logsumexp(jnp.concatenate([words, cluster_logits], 1), axis=1)
        middle_logits = jnp.dot(middle_rows, table_middle.T, preferred_element_type=jnp.float32)
        middle_total = jax.nn.logsumexp(middle_logits, axis=1)
        tail_logits = jnp.dot(tail_rows, table_tail.T, preferred_element_type=jnp.float32)
        tail_total = jax.nn.logsumexp(tail_logits, axis=1)
        pick_head = jnp.take_along_axis(words, jnp.clip(goal, 0, V0 - 1)[:, None], 1)[:, 0]
        pick_middle = jnp.take_along_axis(middle_logits, jnp.clip(goal - V0, 0, V1 - 1)[:, None], 1)[:, 0]
        pick_tail = jnp.take_along_axis(tail_logits, jnp.clip(goal - V0 - V1, 0, V2 - 1)[:, None], 1)[:, 0]
        loss_head = head_total - pick_head
        loss_middle = head_total - cluster_logits[:, 0] + middle_total - pick_middle
        loss_tail = head_total - cluster_logits[:, 1] + tail_total - pick_tail
        return jnp.where(goal < V0, loss_head, jnp.where(goal < V0 + V1, loss_middle, loss_tail))
    losses = lax.map(segment_loss, segment_ids).reshape(SEG * N_CTX)
    return (hidden_out, losses)
```

```python
import jax
import jax.numpy as jnp
from jax import lax
from jax.experimental import pallas as pl
from jax.experimental.pallas import tpu as pltpu
from jax.sharding import PartitionSpec as P

HD = 96
NEG_FILL = -1e30
EPS = 1e-06
F32 = jnp.float32
BF16 = jnp.bfloat16


def norm_full(rows, gain):
    wide = rows.astype(F32)
    mean_sq = jnp.mean(wide * wide, axis=1, keepdims=True)
    return (wide * lax.rsqrt(mean_sq + EPS) * gain[None]).astype(BF16)


def project(full_rows, weight):
    return jnp.dot(full_rows, weight, preferred_element_type=F32).astype(BF16)


def chunk_of(rows):
    best = rows
    if rows > 1024:
        for size in range(16, 1025, 16):
            if rows % size == 0:
                best = size
    return best


def band_stats(band, table_ref, goal):
    rows = table_ref.shape[0]
    chunk = chunk_of(rows)
    top = total = pick = None
    for start in range(0, rows, chunk):
        logits = lax.dot_general(
            table_ref[start : start + chunk, :],
            band,
            (((1,), (1,)), ((), ())),
            preferred_element_type=F32,
        )
        word = lax.broadcasted_iota(jnp.int32, logits.shape, 0)
        chosen = jnp.sum(jnp.where(word == goal - start, logits, 0.0), 0, keepdims=True)
        peak = jnp.max(logits, 0, keepdims=True)
        if top is None:
            top = peak
            total = jnp.sum(jnp.exp(logits - top), 0, keepdims=True)
            pick = chosen
        else:
            higher = jnp.maximum(top, peak)
            total = total * jnp.exp(top - higher) + jnp.sum(
                jnp.exp(logits - higher), 0, keepdims=True
            )
            top = higher
            pick = pick + chosen
    return top, total, pick


def stats_kernel(bands_ref, goals_ref, head_ref, middle_ref, tail_ref, out_ref):
    first = head_ref.shape[1]
    second = first + middle_ref.shape[1]
    one = band_stats(bands_ref[:, :first], head_ref, goals_ref[0:1, :])
    two = band_stats(bands_ref[:, first:second], middle_ref, goals_ref[1:2, :])
    three = band_stats(bands_ref[:, second:], tail_ref, goals_ref[2:3, :])
    out_ref[0:1, :] = one[0]
    out_ref[1:2, :] = one[1]
    out_ref[2:3, :] = two[0]
    out_ref[3:4, :] = two[1]
    out_ref[4:5, :] = three[0]
    out_ref[5:6, :] = three[1]
    out_ref[6:7, :] = one[2] + two[2] + three[2]
    out_ref[7:8, :] = jnp.zeros_like(one[0])


def logit_stats(bands, goals, table_head, table_middle, table_tail):
    tokens, width = bands.shape
    block = 256

    def whole(a):
        return pl.BlockSpec(a.shape, lambda i: (0, 0))

    return pl.pallas_call(
        stats_kernel,
        grid=(tokens // block,),
        in_specs=[
            pl.BlockSpec((block, width), lambda i: (i, 0)),
            pl.BlockSpec((8, block), lambda i: (0, i)),
            whole(table_head),
            whole(table_middle),
            whole(table_tail),
        ],
        out_specs=pl.BlockSpec((8, block), lambda i: (0, i)),
        out_shape=jax.ShapeDtypeStruct((8, tokens), F32),
        compiler_params=pltpu.CompilerParams(vmem_limit_bytes=48 * 1024 * 1024),
    )(bands, goals, table_head, table_middle, table_tail)


def body(
    hidden_in,
    norm_gain,
    w_query,
    w_key,
    w_value,
    w_out,
    head_gain,
    proj_head,
    proj_middle,
    proj_tail,
    table_head,
    table_middle,
    table_tail,
    clusters,
    targets,
):
    seg_len, local_width = hidden_in.shape
    tp_rank = lax.axis_index("tp")
    ctx_rank = lax.axis_index("ctx")
    tp_count = lax.axis_size("tp")
    ctx_count = lax.axis_size("ctx")
    model_width = local_width * tp_count
    v0 = table_head.shape[0] * tp_count * ctx_count
    v1 = table_middle.shape[0] * tp_count * ctx_count

    before = lax.ppermute(hidden_in, "ctx", [(i, i + 1) for i in range(ctx_count - 1)])
    own_full = norm_full(lax.all_gather(hidden_in, "tp", axis=1, tiled=True), norm_gain)
    before_full = norm_full(lax.all_gather(before, "tp", axis=1, tiled=True), norm_gain)
    goals_all = lax.all_gather(targets, "ctx", axis=0, tiled=True)

    queries = project(own_full, w_query)
    keys = jnp.concatenate([project(before_full, w_key), project(own_full, w_key)], 0)
    values = jnp.concatenate([project(before_full, w_value), project(own_full, w_value)], 0)
    heads_local = queries.shape[1] // HD
    query_heads = queries.reshape(seg_len, heads_local, HD)
    key_heads = keys.reshape(2 * seg_len, heads_local, HD)
    value_heads = values.reshape(2 * seg_len, heads_local, HD)
    scores = jnp.einsum(
        "qhe,khe->hqk", query_heads, key_heads, preferred_element_type=F32
    ) * HD ** (-0.5)
    row_pos = lax.broadcasted_iota(jnp.int32, (seg_len, 2 * seg_len), 0)
    col_pos = lax.broadcasted_iota(jnp.int32, (seg_len, 2 * seg_len), 1)
    allowed = jnp.where(col_pos < seg_len, ctx_rank > 0, col_pos - seg_len <= row_pos)
    scores = jnp.where(allowed[None], scores, NEG_FILL)
    top_score = jnp.max(scores, axis=2, keepdims=True)
    raised = jnp.exp(scores - top_score)
    weights = (raised / jnp.sum(raised, axis=2, keepdims=True)).astype(BF16)
    context = jnp.einsum("hqk,khe->qhe", weights, value_heads, preferred_element_type=F32)
    context = context.astype(BF16).reshape(seg_len, heads_local * HD)
    partial_out = jnp.dot(context, w_out, preferred_element_type=F32).astype(BF16)
    attention = lax.psum_scatter(partial_out, "tp", scatter_dimension=1, tiled=True)
    summed = hidden_in.astype(F32) + attention.astype(F32)
    hidden_out = summed.astype(BF16)

    gain_out = lax.dynamic_slice_in_dim(head_gain, tp_rank * local_width, local_width)
    square_sums = lax.psum(jnp.sum(summed * summed, 1), "tp")
    row_scale = lax.rsqrt(square_sums / model_width + EPS)
    scaled = (summed * row_scale[:, None] * gain_out).astype(BF16)
    projection = jnp.concatenate([proj_head, proj_middle, proj_tail], 1)
    partial_bands = jnp.dot(scaled, projection, preferred_element_type=F32).astype(BF16)
    own_bands = lax.psum_scatter(partial_bands, "tp", scatter_dimension=0, tiled=True)
    bands = lax.all_gather(own_bands, ("ctx", "tp"), axis=0, tiled=True)

    place = tp_rank * ctx_count + ctx_rank
    goals = jnp.stack(
        [
            goals_all - place * table_head.shape[0],
            goals_all - v0 - place * table_middle.shape[0],
            goals_all - v0 - v1 - place * table_tail.shape[0],
        ]
        + [jnp.zeros_like(goals_all)] * 5
    )
    stats = logit_stats(bands, goals, table_head, table_middle, table_tail)
    shared = lax.all_to_all(
        stats.reshape(8, ctx_count, seg_len), "ctx", split_axis=1, concat_axis=1, tiled=True
    )
    merged = lax.all_gather(shared, "tp", axis=1, tiled=True)

    def total_of(top, part):
        peak = jnp.max(top, 0)
        return peak + jnp.log(jnp.sum(part * jnp.exp(top - peak[None]), 0))

    head_words = total_of(merged[0], merged[1])
    middle_total = total_of(merged[2], merged[3])
    tail_total = total_of(merged[4], merged[5])
    pick = jnp.sum(merged[6], 0)
    own_rows = lax.dynamic_slice_in_dim(bands, ctx_rank * seg_len, seg_len)
    cluster_logits = lax.dot_general(
        clusters,
        own_rows[:, : clusters.shape[1]],
        (((1,), (1,)), ((), ())),
        preferred_element_type=F32,
    )
    first_cluster, second_cluster = cluster_logits[0], cluster_logits[1]
    highest = jnp.maximum(head_words, jnp.maximum(first_cluster, second_cluster))
    head_total = highest + jnp.log(
        jnp.exp(head_words - highest)
        + jnp.exp(first_cluster - highest)
        + jnp.exp(second_cluster - highest)
    )
    extra = jnp.where(
        targets < v0,
        0.0,
        jnp.where(targets < v0 + v1, middle_total - first_cluster, tail_total - second_cluster),
    )
    return (hidden_out, head_total + extra - pick)


def solution(mesh):
    placed = (
        P("ctx", "tp"),
        P(),
        P(None, "tp"),
        P(None, "tp"),
        P(None, "tp"),
        P("tp", None),
        P(),
        P("tp", None),
        P("tp", None),
        P("tp", None),
        P(("tp", "ctx"), None),
        P(("tp", "ctx"), None),
        P(("tp", "ctx"), None),
        P(),
        P("ctx"),
    )
    return jax.shard_map(
        body, mesh=mesh, in_specs=placed, out_specs=(P("ctx", "tp"), P("ctx")), check_vma=False
    )
```

```python
import functools

import jax
import jax.numpy as jnp
from jax import lax
from jax.experimental import pallas as pl
from jax.experimental.pallas import tpu as pltpu
from jax.sharding import PartitionSpec as P

HD = 96
NEG_FILL = -1e30
EPS = 1e-06
F32 = jnp.float32
BF16 = jnp.bfloat16


def norm_full(rows, gain):
    wide = rows.astype(F32)
    mean_sq = jnp.mean(wide * wide, axis=1, keepdims=True)
    return (wide * lax.rsqrt(mean_sq + EPS) * gain[None]).astype(BF16)


def project(full_rows, weight):
    return jnp.dot(full_rows, weight, preferred_element_type=F32).astype(BF16)


def chunk_of(rows):
    best = rows
    if rows > 1024:
        for size in range(16, 1025, 16):
            if rows % size == 0:
                best = size
    return best


def band_stats(band, table_ref, goal):
    rows = table_ref.shape[0]
    chunk = chunk_of(rows)
    top = total = pick = None
    for start in range(0, rows, chunk):
        logits = lax.dot_general(
            table_ref[start : start + chunk, :],
            band,
            (((1,), (1,)), ((), ())),
            preferred_element_type=F32,
        )
        word = lax.broadcasted_iota(jnp.int32, logits.shape, 0)
        chosen = jnp.sum(jnp.where(word == goal - start, logits, 0.0), 0, keepdims=True)
        peak = jnp.max(logits, 0, keepdims=True)
        if top is None:
            top = peak
            total = jnp.sum(jnp.exp(logits - top), 0, keepdims=True)
            pick = chosen
        else:
            higher = jnp.maximum(top, peak)
            total = total * jnp.exp(top - higher) + jnp.sum(
                jnp.exp(logits - higher), 0, keepdims=True
            )
            top = higher
            pick = pick + chosen
    return top, total, pick


MESH = pl.DeviceIdType.MESH


def tp_device(rank):
    return {"ctx": lax.axis_index("ctx"), "tp": rank}


def remote(src, dst, send_sem, recv_sem, device):
    return pltpu.make_async_remote_copy(
        src_ref=src,
        dst_ref=dst,
        send_sem=send_sem,
        recv_sem=recv_sem,
        device_id=device,
        device_id_type=MESH,
    )


def reduce_kernel(
    tp_count,
    model_width,
    context_ref,
    w_out_ref,
    hidden_ref,
    gain_ref,
    proj_head_ref,
    proj_middle_ref,
    proj_tail_ref,
    hidden_out_ref,
    own_ref,
    a_send,
    a_recv,
    b_send,
    b_recv,
    part,
    c_recv,
    d_send,
    d_recv,
    sq_part,
    sq_recv,
    a_sems,
    b_sems,
    c_sems,
    d_sems,
    sq_sems,
):
    chips = tp_count // 2
    tp = lax.axis_index("tp")
    chip, core = tp // 2, tp % 2
    partner = tp_device(chip * 2 + 1 - core)
    width = hidden_ref.shape[1]
    rows = own_ref.shape[0]

    barrier = pltpu.get_barrier_semaphore()
    for step in range(1, tp_count):
        pl.semaphore_signal(
            barrier, inc=1, device_id=tp_device((tp + step) % tp_count), device_id_type=MESH
        )
    pl.semaphore_wait(barrier, tp_count - 1)

    def columns(rank):
        return pl.ds(pl.multiple_of(rank * width, width), width)

    def tokens(rank):
        return pl.ds(pl.multiple_of(rank * rows, rows), rows)

    context = context_ref[...]
    order = list(range(1, chips)) + [0]
    pending = []
    acc = None
    for j in order:
        there = (chip + j) % chips
        a_send[j] = jnp.dot(
            context, w_out_ref[:, columns(there * 2 + 1 - core)], preferred_element_type=F32
        ).astype(BF16)
        copy = remote(a_send.at[j], a_recv.at[j], a_sems.at[0, j], a_sems.at[1, j], partner)
        copy.start()
        pending.append(copy)
        mine = jnp.dot(
            context, w_out_ref[:, columns(there * 2 + core)], preferred_element_type=F32
        )
        copy.wait_recv()
        mine = mine + a_recv[j].astype(F32)
        if j > 0:
            b_send[j] = mine.astype(BF16)
            copy = remote(
                b_send.at[j],
                b_recv.at[j],
                b_sems.at[0, j],
                b_sems.at[1, j],
                tp_device(there * 2 + core),
            )
            copy.start()
            pending.append(copy)
        else:
            acc = mine
    for j in range(1, chips):
        remote(b_send.at[j], b_recv.at[j], b_sems.at[0, j], b_sems.at[1, j], partner).wait_recv()
        acc = acc + b_recv[j].astype(F32)
    summed = hidden_ref[...].astype(F32) + acc
    hidden_out_ref[...] = summed.astype(BF16)
    squares = jnp.sum(summed * summed, 1, keepdims=True)
    sq_part[...] = jnp.broadcast_to(squares, sq_part.shape)
    for step in range(1, tp_count):
        there = (tp + step) % tp_count
        copy = remote(
            sq_part.at[tokens(there), :],
            sq_recv.at[step],
            sq_sems.at[0, step],
            sq_sems.at[1, step],
            tp_device(there),
        )
        copy.start()
        pending.append(copy)

    scaled = (summed * gain_ref[...]).astype(BF16)
    first = proj_head_ref.shape[1]
    second = first + proj_middle_ref.shape[1]
    part[:, :first] = jnp.dot(scaled, proj_head_ref[...], preferred_element_type=F32).astype(BF16)
    part[:, first:second] = jnp.dot(
        scaled, proj_middle_ref[...], preferred_element_type=F32
    ).astype(BF16)
    part[:, second:] = jnp.dot(scaled, proj_tail_ref[...], preferred_element_type=F32).astype(BF16)
    for j in order:
        there = (chip + j) % chips
        copy = remote(
            part.at[tokens(there * 2 + 1 - core), :],
            c_recv.at[j],
            c_sems.at[0, j],
            c_sems.at[1, j],
            partner,
        )
        copy.start()
        pending.append(copy)
    acc = None
    for j in order:
        there = (chip + j) % chips
        remote(
            part.at[tokens(there * 2 + 1 - core), :],
            c_recv.at[j],
            c_sems.at[0, j],
            c_sems.at[1, j],
            partner,
        ).wait_recv()
        mine = part[tokens(there * 2 + core), :].astype(F32) + c_recv[j].astype(F32)
        if j > 0:
            d_send[j] = mine.astype(BF16)
            copy = remote(
                d_send.at[j],
                d_recv.at[j],
                d_sems.at[0, j],
                d_sems.at[1, j],
                tp_device(there * 2 + core),
            )
            copy.start()
            pending.append(copy)
        else:
            acc = mine
    total_sq = sq_part[tokens(tp), :]
    for step in range(1, tp_count):
        remote(
            sq_part.at[tokens(tp), :],
            sq_recv.at[step],
            sq_sems.at[0, step],
            sq_sems.at[1, step],
            partner,
        ).wait_recv()
        total_sq = total_sq + sq_recv[step]
    row_scale = lax.rsqrt(total_sq[:, :1] / model_width + EPS)
    for j in range(1, chips):
        remote(d_send.at[j], d_recv.at[j], d_sems.at[0, j], d_sems.at[1, j], partner).wait_recv()
        acc = acc + d_recv[j].astype(F32)
    own_ref[...] = (acc * row_scale).astype(BF16)
    for copy in pending:
        copy.wait_send()


def reduced_bands(context, w_out, hidden_in, gain, proj_head, proj_middle, proj_tail):
    tp_count = lax.axis_size("tp")
    chips = tp_count // 2
    tokens, width = hidden_in.shape
    rows = tokens // tp_count
    bands = proj_head.shape[1] + proj_middle.shape[1] + proj_tail.shape[1]
    return pl.pallas_call(
        functools.partial(reduce_kernel, tp_count, width * tp_count),
        out_shape=(
            jax.ShapeDtypeStruct((tokens, width), BF16),
            jax.ShapeDtypeStruct((rows, bands), BF16),
        ),
        in_specs=[pl.BlockSpec(memory_space=pltpu.VMEM)] * 7,
        out_specs=(pl.BlockSpec(memory_space=pltpu.VMEM),) * 2,
        scratch_shapes=[pltpu.VMEM((chips, tokens, width), BF16)] * 4
        + [pltpu.VMEM((tokens, bands), BF16)]
        + [pltpu.VMEM((chips, rows, bands), BF16)] * 3
        + [pltpu.VMEM((tokens, 128), F32), pltpu.VMEM((tp_count, rows, 128), F32)]
        + [pltpu.SemaphoreType.DMA((2, chips))] * 4
        + [pltpu.SemaphoreType.DMA((2, tp_count))],
        compiler_params=pltpu.CompilerParams(
            collective_id=0, has_side_effects=True, vmem_limit_bytes=48 * 1024 * 1024
        ),
    )(context, w_out, hidden_in, gain, proj_head, proj_middle, proj_tail)


def combined(one, other):
    top = jnp.maximum(one[0], other[0])
    return (
        top,
        one[1] * jnp.exp(one[0] - top) + other[1] * jnp.exp(other[0] - top),
        one[2] + other[2],
    )


def loss_kernel(
    line,
    tp_count,
    own_ref,
    targets_ref,
    clusters_ref,
    head_ref,
    head_pair_ref,
    middle_ref,
    middle_pair_ref,
    tail_ref,
    tail_pair_ref,
    losses_ref,
    bands,
    goals,
    stat_send,
    stat_recv,
    z_send,
    z_recv,
    y_sems,
    c_sems,
    g_sems,
    s_sems,
):
    chips = tp_count // 2
    tp = lax.axis_index("tp")
    ctx = lax.axis_index("ctx")
    chip, core = tp // 2, tp % 2
    spot, side = ctx // 2, ctx % 2
    rows = own_ref.shape[0]
    ctx_count = line * 2
    v0 = head_ref.shape[0] * tp_count * ctx_count
    v1 = middle_ref.shape[0] * tp_count * ctx_count

    def device(place, rank):
        return {"ctx": place * 2 + side, "tp": rank}

    barrier = pltpu.get_barrier_semaphore()
    for k in range(line):
        for t in range(tp_count):
            if k or t:
                pl.semaphore_signal(
                    barrier,
                    inc=1,
                    device_id=device((spot + k) % line, (tp + t) % tp_count),
                    device_id_type=MESH,
                )
    pl.semaphore_wait(barrier, line * tp_count - 1)

    def shard(source, rank):
        return bands.at[source, pl.ds(pl.multiple_of(rank * rows, rows), rows), :]

    def along(d, source, way):
        there = spot + 1 if way == 0 else spot - 1
        piece = shard(source, tp)
        return remote(
            piece, piece, z_send.at[way, d], z_recv.at[way, d + 1], device(there, tp)
        )

    def arrival(d, source, way):
        piece = shard(source, tp)
        return remote(piece, piece, z_send.at[way, d], z_recv.at[way, d], device(spot, tp))

    def sideways(source, j):
        piece = shard(source, tp)
        there = ((chip + j) % chips) * 2 + core
        return remote(
            piece, piece, y_sems.at[0, source, j], y_sems.at[1, source, j], device(spot, there)
        )

    def from_side(source, j):
        piece = shard(source, ((chip - j + chips) % chips) * 2 + core)
        return remote(
            piece, piece, y_sems.at[0, source, j], y_sems.at[1, source, j], device(spot, tp)
        )

    def across(source, j, owner_core):
        piece = shard(source, ((chip - j + chips) % chips) * 2 + owner_core)
        return remote(
            piece,
            piece,
            c_sems.at[0, source, j],
            c_sems.at[1, source, j],
            device(spot, chip * 2 + 1 - core),
        )

    def spread(source):
        for j in range(1, chips):
            sideways(source, j).start()
        across(source, 0, core).start()

    def goal_copy(k):
        return remote(
            goals.at[spot],
            goals.at[spot],
            g_sems.at[0, k],
            g_sems.at[1, k],
            device((spot + k) % line, tp),
        )

    def stat_copy(source, t):
        return remote(
            stat_send.at[source],
            stat_recv.at[spot * tp_count + tp],
            s_sems.at[0, source, t],
            s_sems.at[1, spot, t],
            device(source, (tp + t) % tp_count),
        )

    bands[spot, pl.ds(pl.multiple_of(tp * rows, rows), rows), :] = own_ref[...]
    goals[spot] = targets_ref[...]

    @pl.when(spot + 1 < line)
    def _():
        along(0, spot, 0).start()

    @pl.when(spot > 0)
    def _():
        along(0, spot, 1).start()

    spread(spot)
    for k in range(1, line):
        goal_copy(k).start()
    for k in range(1, line):
        place = (spot - k + line) % line
        remote(
            goals.at[place], goals.at[place], g_sems.at[0, k], g_sems.at[1, k], device(spot, tp)
        ).wait_recv()

    place_own = tp * ctx_count + ctx
    place_pair = tp * ctx_count + spot * 2 + 1 - side
    first = head_ref.shape[1]
    second = first + middle_ref.shape[1]

    def finish(source):
        for j in range(1, chips):
            from_side(source, j).wait_recv()
            across(source, j, core).start()
        for j in range(chips):
            across(source, j, 1 - core).wait_recv()
        goal = goals[source][0:1, :]

        def band(low, high, base, own, pair):
            size = own.shape[0]
            piece = bands[source, :, low:high]
            return combined(
                band_stats(piece, own, goal - base - place_own * size),
                band_stats(piece, pair, goal - base - place_pair * size),
            )

        one = band(0, first, 0, head_ref, head_pair_ref)
        two = band(first, second, v0, middle_ref, middle_pair_ref)
        three = band(second, bands.shape[2], v0 + v1, tail_ref, tail_pair_ref)
        found = (one[0], one[1], two[0], two[1], three[0], three[1], one[2] + two[2] + three[2])
        for i, value in enumerate(found):
            stat_send[source, i : i + 1, :] = value
        stat_send[source, 7:8, :] = jnp.zeros_like(one[0])
        for t in range(1, tp_count):
            stat_copy(source, t).start()

        @pl.when(source != spot)
        def _():
            stat_copy(source, 0).start()

    def step(d, carry):
        @pl.when((d + 1 < line) & (spot - d - 1 >= 0))
        def _():
            source = spot - d - 1
            arrival(d + 1, source, 0).wait_recv()

            @pl.when(spot + 1 < line)
            def _():
                along(d + 1, source, 0).start()

            spread(source)

        @pl.when((d + 1 < line) & (spot + d + 1 < line))
        def _():
            source = spot + d + 1
            arrival(d + 1, source, 1).wait_recv()

            @pl.when(spot > 0)
            def _():
                along(d + 1, source, 1).start()

            spread(source)

        @pl.when(spot - d >= 0)
        def _():
            finish(spot - d)

        @pl.when((d > 0) & (spot + d < line))
        def _():
            finish(spot + d)

        return carry

    lax.fori_loop(0, line, step, 0)

    stat_recv[spot * tp_count + tp] = stat_send[spot]
    clusters = lax.dot_general(
        clusters_ref[...],
        bands[spot, :, :first],
        (((1,), (1,)), ((), ())),
        preferred_element_type=F32,
    )
    for k in range(line):
        place = (spot + k) % line
        for t in range(tp_count):
            if k or t:
                slot = stat_recv.at[place * tp_count + (tp - t + tp_count) % tp_count]
                remote(
                    slot, slot, s_sems.at[0, place, t], s_sems.at[1, place, t], device(spot, tp)
                ).wait_recv()

    def total_of(i):
        tops = stat_recv[:, i, :]
        top = jnp.max(tops, 0, keepdims=True)
        return top + jnp.log(
            jnp.sum(stat_recv[:, i + 1, :] * jnp.exp(tops - top), 0, keepdims=True)
        )

    words = total_of(0)
    middle_total = total_of(2)
    tail_total = total_of(4)
    pick = jnp.sum(stat_recv[:, 6, :], 0, keepdims=True)
    first_cluster, second_cluster = clusters[0:1, :], clusters[1:2, :]
    top = jnp.maximum(words, jnp.maximum(first_cluster, second_cluster))
    head_total = top + jnp.log(
        jnp.exp(words - top) + jnp.exp(first_cluster - top) + jnp.exp(second_cluster - top)
    )
    goal = targets_ref[0:1, :]
    extra = jnp.where(
        goal < v0,
        0.0,
        jnp.where(goal < v0 + v1, middle_total - first_cluster, tail_total - second_cluster),
    )
    losses_ref[...] = head_total + extra - pick

    for k in range(1, line):
        goal_copy(k).wait_send()

    def settle(source, carry):
        for j in range(1, chips):
            sideways(source, j).wait_send()
        for j in range(chips):
            across(source, j, core).wait_send()
        for t in range(1, tp_count):
            stat_copy(source, t).wait_send()

        @pl.when(source != spot)
        def _():
            stat_copy(source, 0).wait_send()

        @pl.when((spot + 1 < line) & (spot - source >= 0))
        def _():
            along(source, spot - source, 0).wait_send()

        @pl.when((spot > 0) & (spot + source < line))
        def _():
            along(source, spot + source, 1).wait_send()

        return carry

    lax.fori_loop(0, line, settle, 0)


def band_losses(own_bands, targets, clusters, tables):
    tp_count = lax.axis_size("tp")
    ctx_count = lax.axis_size("ctx")
    line = ctx_count // 2
    chips = tp_count // 2
    tokens = targets.shape[0]
    width = own_bands.shape[1]
    swap = [(i, i ^ 1) for i in range(ctx_count)]
    paired = []
    for table in tables:
        paired += [table, lax.ppermute(table, "ctx", swap)]
    goals = jnp.broadcast_to(targets[None], (8, tokens))
    clusters = jnp.pad(clusters, ((0, 16 - clusters.shape[0]), (0, 0)))
    dma = pltpu.SemaphoreType.DMA
    return pl.pallas_call(
        functools.partial(loss_kernel, line, tp_count),
        out_shape=jax.ShapeDtypeStruct((1, tokens), F32),
        in_specs=[pl.BlockSpec(memory_space=pltpu.VMEM)] * 9,
        out_specs=pl.BlockSpec(memory_space=pltpu.VMEM),
        scratch_shapes=[
            pltpu.VMEM((line, tokens, width), BF16),
            pltpu.VMEM((line, 8, tokens), jnp.int32),
            pltpu.VMEM((line, 8, tokens), F32),
            pltpu.VMEM((line * tp_count, 8, tokens), F32),
            dma((2, line + 1)),
            dma((2, line + 1)),
            dma((2, line, chips)),
            dma((2, line, chips)),
            dma((2, line)),
            dma((2, line, tp_count)),
        ],
        compiler_params=pltpu.CompilerParams(
            collective_id=1, has_side_effects=True, vmem_limit_bytes=52 * 1024 * 1024
        ),
    )(own_bands, goals, clusters, *paired)[0]


def body(
    hidden_in,
    norm_gain,
    w_query,
    w_key,
    w_value,
    w_out,
    head_gain,
    proj_head,
    proj_middle,
    proj_tail,
    table_head,
    table_middle,
    table_tail,
    clusters,
    targets,
):
    seg_len, local_width = hidden_in.shape
    tp_rank = lax.axis_index("tp")
    ctx_rank = lax.axis_index("ctx")
    ctx_count = lax.axis_size("ctx")

    before = lax.ppermute(hidden_in, "ctx", [(i, i + 1) for i in range(ctx_count - 1)])
    own_full = norm_full(lax.all_gather(hidden_in, "tp", axis=1, tiled=True), norm_gain)
    before_full = norm_full(lax.all_gather(before, "tp", axis=1, tiled=True), norm_gain)

    queries = project(own_full, w_query)
    keys = jnp.concatenate([project(before_full, w_key), project(own_full, w_key)], 0)
    values = jnp.concatenate([project(before_full, w_value), project(own_full, w_value)], 0)
    heads_local = queries.shape[1] // HD
    query_heads = queries.reshape(seg_len, heads_local, HD)
    key_heads = keys.reshape(2 * seg_len, heads_local, HD)
    value_heads = values.reshape(2 * seg_len, heads_local, HD)
    scores = jnp.einsum(
        "qhe,khe->hqk", query_heads, key_heads, preferred_element_type=F32
    ) * HD ** (-0.5)
    row_pos = lax.broadcasted_iota(jnp.int32, (seg_len, 2 * seg_len), 0)
    col_pos = lax.broadcasted_iota(jnp.int32, (seg_len, 2 * seg_len), 1)
    allowed = jnp.where(col_pos < seg_len, ctx_rank > 0, col_pos - seg_len <= row_pos)
    scores = jnp.where(allowed[None], scores, NEG_FILL)
    top_score = jnp.max(scores, axis=2, keepdims=True)
    raised = jnp.exp(scores - top_score)
    weights = (raised / jnp.sum(raised, axis=2, keepdims=True)).astype(BF16)
    context = jnp.einsum("hqk,khe->qhe", weights, value_heads, preferred_element_type=F32)
    context = context.astype(BF16).reshape(seg_len, heads_local * HD)
    gain_out = lax.dynamic_slice_in_dim(head_gain, tp_rank * local_width, local_width)
    hidden_out, own_bands = reduced_bands(
        context, w_out, hidden_in, gain_out[None], proj_head, proj_middle, proj_tail
    )
    losses = band_losses(
        own_bands, targets, clusters, (table_head, table_middle, table_tail)
    )
    return (hidden_out, losses)


def solution(mesh):
    placed = (
        P("ctx", "tp"),
        P(),
        P(None, "tp"),
        P(None, "tp"),
        P(None, "tp"),
        P("tp", None),
        P(),
        P("tp", None),
        P("tp", None),
        P("tp", None),
        P(("tp", "ctx"), None),
        P(("tp", "ctx"), None),
        P(("tp", "ctx"), None),
        P(),
        P("ctx"),
    )
    return jax.shard_map(
        body, mesh=mesh, in_specs=placed, out_specs=(P("ctx", "tp"), P("ctx")), check_vma=False
    )
```

```python
import functools

import jax
import jax.numpy as jnp
from jax import lax
from jax.experimental import pallas as pl
from jax.experimental.pallas import tpu as pltpu
from jax.sharding import PartitionSpec as P

HD = 96
NEG_FILL = -1e30
EPS = 1e-06
F32 = jnp.float32
BF16 = jnp.bfloat16


def chunk_of(rows):
    best = rows
    if rows > 1024:
        for size in range(16, 1025, 16):
            if rows % size == 0:
                best = size
    return best


def band_stats(band, table_ref, goal):
    rows = table_ref.shape[0]
    chunk = chunk_of(rows)
    top = total = pick = None
    for start in range(0, rows, chunk):
        logits = lax.dot_general(
            table_ref[start : start + chunk, :],
            band,
            (((1,), (1,)), ((), ())),
            preferred_element_type=F32,
        )
        word = lax.broadcasted_iota(jnp.int32, logits.shape, 0)
        chosen = jnp.sum(jnp.where(word == goal - start, logits, 0.0), 0, keepdims=True)
        peak = jnp.max(logits, 0, keepdims=True)
        if top is None:
            top = peak
            total = jnp.sum(jnp.exp(logits - top), 0, keepdims=True)
            pick = chosen
        else:
            higher = jnp.maximum(top, peak)
            total = total * jnp.exp(top - higher) + jnp.sum(
                jnp.exp(logits - higher), 0, keepdims=True
            )
            top = higher
            pick = pick + chosen
    return top, total, pick


MESH = pl.DeviceIdType.MESH


def tp_device(rank):
    return {"ctx": lax.axis_index("ctx"), "tp": rank}


def remote(src, dst, send_sem, recv_sem, device):
    return pltpu.make_async_remote_copy(
        src_ref=src,
        dst_ref=dst,
        send_sem=send_sem,
        recv_sem=recv_sem,
        device_id=device,
        device_id_type=MESH,
    )


def reduce_phase(
    tp_count,
    model_width,
    context_ref,
    w_out_ref,
    hidden_ref,
    gain_ref,
    proj_refs,
    hidden_out_ref,
    own_ref,
    buffers,
    sems,
    loads,
):
    a_send, a_recv, b_send, b_recv, part, c_recv, d_send, d_recv, sq_part, sq_recv = buffers
    a_sems, b_sems, c_sems, d_sems, sq_sems = sems
    proj_head_ref, proj_middle_ref, proj_tail_ref = proj_refs
    chips = tp_count // 2
    tp = lax.axis_index("tp")
    chip, core = tp // 2, tp % 2
    partner = tp_device(chip * 2 + 1 - core)
    width = hidden_ref.shape[1]
    rows = own_ref.shape[0]

    def columns(rank):
        return pl.ds(pl.multiple_of(rank * width, width), width)

    def tokens(rank):
        return pl.ds(pl.multiple_of(rank * rows, rows), rows)

    loads[0].wait()
    context = context_ref[...]
    order = list(range(1, chips)) + [0]
    pending = []
    acc = None
    for j in order:
        there = (chip + j) % chips
        a_send[j] = jnp.dot(
            context, w_out_ref[:, columns(there * 2 + 1 - core)], preferred_element_type=F32
        ).astype(BF16)
        copy = remote(a_send.at[j], a_recv.at[j], a_sems.at[0, j], a_sems.at[1, j], partner)
        copy.start()
        pending.append(copy)
        mine = jnp.dot(
            context, w_out_ref[:, columns(there * 2 + core)], preferred_element_type=F32
        )
        copy.wait_recv()
        mine = mine + a_recv[j].astype(F32)
        if j > 0:
            b_send[j] = mine.astype(BF16)
            copy = remote(
                b_send.at[j],
                b_recv.at[j],
                b_sems.at[0, j],
                b_sems.at[1, j],
                tp_device(there * 2 + core),
            )
            copy.start()
            pending.append(copy)
        else:
            acc = mine
    for j in range(1, chips):
        remote(b_send.at[j], b_recv.at[j], b_sems.at[0, j], b_sems.at[1, j], partner).wait_recv()
        acc = acc + b_recv[j].astype(F32)
    summed = hidden_ref[...].astype(F32) + acc
    hidden_out_ref[...] = summed.astype(BF16)
    squares = jnp.sum(summed * summed, 1, keepdims=True)
    sq_part[...] = jnp.broadcast_to(squares, sq_part.shape)
    for step in range(1, tp_count):
        there = (tp + step) % tp_count
        copy = remote(
            sq_part.at[tokens(there), :],
            sq_recv.at[step],
            sq_sems.at[0, step],
            sq_sems.at[1, step],
            tp_device(there),
        )
        copy.start()
        pending.append(copy)

    scaled = (summed * gain_ref[:, columns(tp)]).astype(BF16)
    for load in loads[1:]:
        load.wait()
    first = proj_head_ref.shape[1]
    second = first + proj_middle_ref.shape[1]
    part[:, :first] = jnp.dot(scaled, proj_head_ref[...], preferred_element_type=F32).astype(BF16)
    part[:, first:second] = jnp.dot(
        scaled, proj_middle_ref[...], preferred_element_type=F32
    ).astype(BF16)
    part[:, second:] = jnp.dot(scaled, proj_tail_ref[...], preferred_element_type=F32).astype(BF16)
    for j in order:
        there = (chip + j) % chips
        copy = remote(
            part.at[tokens(there * 2 + 1 - core), :],
            c_recv.at[j],
            c_sems.at[0, j],
            c_sems.at[1, j],
            partner,
        )
        copy.start()
        pending.append(copy)
    acc = None
    for j in order:
        there = (chip + j) % chips
        remote(
            part.at[tokens(there * 2 + 1 - core), :],
            c_recv.at[j],
            c_sems.at[0, j],
            c_sems.at[1, j],
            partner,
        ).wait_recv()
        mine = part[tokens(there * 2 + core), :].astype(F32) + c_recv[j].astype(F32)
        if j > 0:
            d_send[j] = mine.astype(BF16)
            copy = remote(
                d_send.at[j],
                d_recv.at[j],
                d_sems.at[0, j],
                d_sems.at[1, j],
                tp_device(there * 2 + core),
            )
            copy.start()
            pending.append(copy)
        else:
            acc = mine
    total_sq = sq_part[tokens(tp), :]
    for step in range(1, tp_count):
        remote(
            sq_part.at[tokens(tp), :],
            sq_recv.at[step],
            sq_sems.at[0, step],
            sq_sems.at[1, step],
            partner,
        ).wait_recv()
        total_sq = total_sq + sq_recv[step]
    row_scale = lax.rsqrt(total_sq[:, :1] / model_width + EPS)
    for j in range(1, chips):
        remote(d_send.at[j], d_recv.at[j], d_sems.at[0, j], d_sems.at[1, j], partner).wait_recv()
        acc = acc + d_recv[j].astype(F32)
    own_ref[...] = (acc * row_scale).astype(BF16)
    for copy in pending:
        copy.wait_send()


def combined(one, other):
    top = jnp.maximum(one[0], other[0])
    return (
        top,
        one[1] * jnp.exp(one[0] - top) + other[1] * jnp.exp(other[0] - top),
        one[2] + other[2],
    )


def loss_phase(
    line,
    tp_count,
    own_ref,
    targets_ref,
    clusters_ref,
    table_refs,
    losses_ref,
    buffers,
    sems,
    loads,
    swaps,
):
    head_ref, head_pair_ref, middle_ref, middle_pair_ref, tail_ref, tail_pair_ref = table_refs
    bands, goals, stat_send, stat_recv = buffers
    z_send, z_recv, y_sems, c_sems, g_sems, s_sems = sems
    chips = tp_count // 2
    tp = lax.axis_index("tp")
    ctx = lax.axis_index("ctx")
    chip, core = tp // 2, tp % 2
    spot, side = ctx // 2, ctx % 2
    rows = own_ref.shape[0]
    ctx_count = line * 2
    v0 = head_ref.shape[0] * tp_count * ctx_count
    v1 = middle_ref.shape[0] * tp_count * ctx_count

    def device(place, rank):
        return {"ctx": place * 2 + side, "tp": rank}

    def shard(source, rank):
        return bands.at[source, pl.ds(pl.multiple_of(rank * rows, rows), rows), :]

    def along(d, source, way):
        there = spot + 1 if way == 0 else spot - 1
        piece = shard(source, tp)
        return remote(
            piece, piece, z_send.at[way, d], z_recv.at[way, d + 1], device(there, tp)
        )

    def arrival(d, source, way):
        piece = shard(source, tp)
        return remote(piece, piece, z_send.at[way, d], z_recv.at[way, d], device(spot, tp))

    def sideways(source, j):
        piece = shard(source, tp)
        there = ((chip + j) % chips) * 2 + core
        return remote(
            piece, piece, y_sems.at[0, source, j], y_sems.at[1, source, j], device(spot, there)
        )

    def from_side(source, j):
        piece = shard(source, ((chip - j + chips) % chips) * 2 + core)
        return remote(
            piece, piece, y_sems.at[0, source, j], y_sems.at[1, source, j], device(spot, tp)
        )

    def across(source, j, owner_core):
        piece = shard(source, ((chip - j + chips) % chips) * 2 + owner_core)
        return remote(
            piece,
            piece,
            c_sems.at[0, source, j],
            c_sems.at[1, source, j],
            device(spot, chip * 2 + 1 - core),
        )

    def spread(source):
        for j in range(1, chips):
            sideways(source, j).start()
        across(source, 0, core).start()

    def goal_copy(k):
        return remote(
            goals.at[spot],
            goals.at[spot],
            g_sems.at[0, k],
            g_sems.at[1, k],
            device((spot + k) % line, tp),
        )

    def stat_copy(source, t):
        return remote(
            stat_send.at[source],
            stat_recv.at[spot * tp_count + tp],
            s_sems.at[0, source, t],
            s_sems.at[1, spot, t],
            device(source, (tp + t) % tp_count),
        )

    bands[spot, pl.ds(pl.multiple_of(tp * rows, rows), rows), :] = own_ref[...]
    goals[spot] = targets_ref[...]

    @pl.when(spot + 1 < line)
    def _():
        along(0, spot, 0).start()

    @pl.when(spot > 0)
    def _():
        along(0, spot, 1).start()

    spread(spot)
    for k in range(1, line):
        goal_copy(k).start()
    for k in range(1, line):
        place = (spot - k + line) % line
        remote(
            goals.at[place], goals.at[place], g_sems.at[0, k], g_sems.at[1, k], device(spot, tp)
        ).wait_recv()

    for load in loads:
        load.wait()
    for swap in swaps:
        swap.wait()
    place_own = tp * ctx_count + ctx
    place_pair = tp * ctx_count + spot * 2 + 1 - side
    first = head_ref.shape[1]
    second = first + middle_ref.shape[1]

    def finish(source):
        for j in range(1, chips):
            from_side(source, j).wait_recv()
            across(source, j, core).start()
        for j in range(chips):
            across(source, j, 1 - core).wait_recv()
        goal = goals[source][0:1, :]

        def band(low, high, base, own, pair):
            size = own.shape[0]
            piece = bands[source, :, low:high]
            return combined(
                band_stats(piece, own, goal - base - place_own * size),
                band_stats(piece, pair, goal - base - place_pair * size),
            )

        one = band(0, first, 0, head_ref, head_pair_ref)
        two = band(first, second, v0, middle_ref, middle_pair_ref)
        three = band(second, bands.shape[2], v0 + v1, tail_ref, tail_pair_ref)
        found = (one[0], one[1], two[0], two[1], three[0], three[1], one[2] + two[2] + three[2])
        for i, value in enumerate(found):
            stat_send[source, i : i + 1, :] = value
        stat_send[source, 7:8, :] = jnp.zeros_like(one[0])
        for t in range(1, tp_count):
            stat_copy(source, t).start()

        @pl.when(source != spot)
        def _():
            stat_copy(source, 0).start()

    def step(d, carry):
        @pl.when((d + 1 < line) & (spot - d - 1 >= 0))
        def _():
            source = spot - d - 1
            arrival(d + 1, source, 0).wait_recv()

            @pl.when(spot + 1 < line)
            def _():
                along(d + 1, source, 0).start()

            spread(source)

        @pl.when((d + 1 < line) & (spot + d + 1 < line))
        def _():
            source = spot + d + 1
            arrival(d + 1, source, 1).wait_recv()

            @pl.when(spot > 0)
            def _():
                along(d + 1, source, 1).start()

            spread(source)

        @pl.when(spot - d >= 0)
        def _():
            finish(spot - d)

        @pl.when((d > 0) & (spot + d < line))
        def _():
            finish(spot + d)

        return carry

    lax.fori_loop(0, line, step, 0)

    stat_recv[spot * tp_count + tp] = stat_send[spot]
    clusters = lax.dot_general(
        clusters_ref[...],
        bands[spot, :, :first],
        (((1,), (1,)), ((), ())),
        preferred_element_type=F32,
    )
    for k in range(line):
        place = (spot + k) % line
        for t in range(tp_count):
            if k or t:
                slot = stat_recv.at[place * tp_count + (tp - t + tp_count) % tp_count]
                remote(
                    slot, slot, s_sems.at[0, place, t], s_sems.at[1, place, t], device(spot, tp)
                ).wait_recv()

    def total_of(i):
        tops = stat_recv[:, i, :]
        top = jnp.max(tops, 0, keepdims=True)
        return top + jnp.log(
            jnp.sum(stat_recv[:, i + 1, :] * jnp.exp(tops - top), 0, keepdims=True)
        )

    words = total_of(0)
    middle_total = total_of(2)
    tail_total = total_of(4)
    pick = jnp.sum(stat_recv[:, 6, :], 0, keepdims=True)
    first_cluster, second_cluster = clusters[0:1, :], clusters[1:2, :]
    top = jnp.maximum(words, jnp.maximum(first_cluster, second_cluster))
    head_total = top + jnp.log(
        jnp.exp(words - top) + jnp.exp(first_cluster - top) + jnp.exp(second_cluster - top)
    )
    goal = targets_ref[0:1, :]
    extra = jnp.where(
        goal < v0,
        0.0,
        jnp.where(goal < v0 + v1, middle_total - first_cluster, tail_total - second_cluster),
    )
    losses_ref[...] = head_total + extra - pick

    for k in range(1, line):
        goal_copy(k).wait_send()

    def settle(source, carry):
        for j in range(1, chips):
            sideways(source, j).wait_send()
        for j in range(chips):
            across(source, j, core).wait_send()
        for t in range(1, tp_count):
            stat_copy(source, t).wait_send()

        @pl.when(source != spot)
        def _():
            stat_copy(source, 0).wait_send()

        @pl.when((spot + 1 < line) & (spot - source >= 0))
        def _():
            along(source, spot - source, 0).wait_send()

        @pl.when((spot > 0) & (spot + source < line))
        def _():
            along(source, spot + source, 1).wait_send()

        return carry

    lax.fori_loop(0, line, settle, 0)


def attention_phase(
    tp_count,
    ctx_count,
    hidden_ref,
    gain_ref,
    weights,
    loads,
    swaps,
    buffers,
    sems,
):
    rows, normed, queries, keys, values, acc, context_ref = buffers
    p_sems, y_sems, c_sems = sems
    chips = tp_count // 2
    tp = lax.axis_index("tp")
    ctx = lax.axis_index("ctx")
    chip, core = tp // 2, tp % 2
    seg_len, width = hidden_ref.shape
    group = 4 * HD

    def shard(part, rank):
        return rows.at[part, :, pl.ds(pl.multiple_of(rank * width, width), width)]

    def sideways(part, j):
        piece = shard(part, tp)
        there = ((chip + j) % chips) * 2 + core
        return remote(
            piece, piece, y_sems.at[0, part, j], y_sems.at[1, part, j], tp_device(there)
        )

    def from_side(part, j):
        piece = shard(part, ((chip - j + chips) % chips) * 2 + core)
        return remote(piece, piece, y_sems.at[0, part, j], y_sems.at[1, part, j], tp_device(tp))

    def across(part, j, owner_core):
        piece = shard(part, ((chip - j + chips) % chips) * 2 + owner_core)
        return remote(
            piece,
            piece,
            c_sems.at[0, part, j],
            c_sems.at[1, part, j],
            tp_device(chip * 2 + 1 - core),
        )

    def spread(part):
        for j in range(1, chips):
            sideways(part, j).start()
        across(part, 0, core).start()

    def relay(part):
        for j in range(1, chips):
            from_side(part, j).wait_recv()
            across(part, j, core).start()

    def normalise(part):
        for j in range(chips):
            across(part, j, 1 - core).wait_recv()
        wide = rows[part].astype(F32)
        mean_sq = jnp.mean(wide * wide, axis=1, keepdims=True)
        normed[...] = (wide * lax.rsqrt(mean_sq + EPS) * gain_ref[...]).astype(BF16)

    def project(weight, out, start):
        def tile(i, carry):
            cut = pl.ds(pl.multiple_of(i * group, group), group)
            out[start : start + seg_len, cut] = jnp.dot(
                normed[...], weight[:, cut], preferred_element_type=F32
            ).astype(BF16)
            return carry

        lax.fori_loop(0, width // group, tile, 0)

    rows[1, :, pl.ds(pl.multiple_of(tp * width, width), width)] = hidden_ref[...]
    forward = remote(
        shard(1, tp),
        shard(0, tp),
        p_sems.at[0],
        p_sems.at[1],
        {"ctx": (ctx + 1) % ctx_count, "tp": tp},
    )
    forward.start()
    spread(1)
    relay(1)
    forward.wait_recv()
    spread(0)
    for swap in swaps:
        swap.start()
    normalise(1)
    for load in loads:
        load.wait()
    project(weights[0], queries, 0)
    project(weights[1], keys, seg_len)
    project(weights[2], values, seg_len)
    relay(0)
    normalise(0)
    project(weights[1], keys, 0)
    project(weights[2], values, 0)

    def heads(i, carry):
        for h in range(4):
            low = h * HD // 128 * 128
            high = -(-(h + 1) * HD // 128) * 128
            cut = pl.ds(pl.multiple_of(i * group + low, 128), high - low)
            lane = lax.broadcasted_iota(jnp.int32, (seg_len, high - low), 1) + low
            inside = (lane >= h * HD) & (lane < (h + 1) * HD)
            query = jnp.where(inside, queries[:, cut].astype(F32), 0.0).astype(BF16)
            scores = lax.dot_general(
                query, keys[:, cut], (((1,), (1,)), ((), ())), preferred_element_type=F32
            ) * HD ** (-0.5)
            row_pos = lax.broadcasted_iota(jnp.int32, scores.shape, 0)
            col_pos = lax.broadcasted_iota(jnp.int32, scores.shape, 1)
            first = jnp.where(ctx > 0, 0, seg_len)
            allowed = (col_pos >= first) & (col_pos - seg_len <= row_pos)
            scores = jnp.where(allowed, scores, NEG_FILL)
            raised = jnp.exp(scores - jnp.max(scores, axis=1, keepdims=True))
            shares = (raised / jnp.sum(raised, axis=1, keepdims=True)).astype(BF16)
            mixed = jnp.dot(shares, values[:, cut], preferred_element_type=F32)
            acc[:, cut] = jnp.where(inside, mixed, acc[:, cut])
        return carry

    acc[...] = jnp.zeros_like(acc)
    lax.fori_loop(0, width // group, heads, 0)
    context_ref[...] = acc[...].astype(BF16)

    forward.wait_send()
    for part in range(2):
        for j in range(1, chips):
            sideways(part, j).wait_send()
        for j in range(chips):
            across(part, j, core).wait_send()


def layer_kernel(line, tp_count, *refs):
    (
        hidden_ref,
        norm_gain_ref,
        head_gain_ref,
        clusters_ref,
        targets_ref,
        wq_ref,
        wk_ref,
        wv_ref,
        wo_ref,
        ph_ref,
        pm_ref,
        pt_ref,
        th_ref,
        tm_ref,
        tt_ref,
        hidden_out_ref,
        losses_ref,
    ) = refs[:17]
    held = refs[17:30]
    weights, proj = held[0:4], held[4:7]
    tables = held[7:13]
    attention = refs[30:37]
    own = refs[37]
    reduce = refs[38:48]
    loss = refs[48:52]
    load_sems, swap_sems = refs[52:54]
    attention_sems = refs[54:57]
    reduce_sems = refs[57:62]
    loss_sems = refs[62:68]
    ctx_count = line * 2
    tp = lax.axis_index("tp")
    ctx = lax.axis_index("ctx")
    spot, side = ctx // 2, ctx % 2

    sources = (wq_ref, wk_ref, wv_ref, wo_ref, ph_ref, pm_ref, pt_ref, th_ref, tm_ref, tt_ref)
    targets = weights + proj + tables[0::2]
    loads = [
        pltpu.make_async_copy(source, target, load_sems.at[i])
        for i, (source, target) in enumerate(zip(sources, targets))
    ]
    for load in loads:
        load.start()

    barrier = pltpu.get_barrier_semaphore()
    peers = [
        {"ctx": ((spot + k) % line) * 2 + side, "tp": (tp + t) % tp_count}
        for k in range(line)
        for t in range(tp_count)
        if k or t
    ]
    peers += [
        {"ctx": (ctx + 1) % ctx_count, "tp": tp},
        {"ctx": (ctx + ctx_count - 1) % ctx_count, "tp": tp},
    ]
    for peer in peers:
        pl.semaphore_signal(barrier, inc=1, device_id=peer, device_id_type=MESH)
    pl.semaphore_wait(barrier, len(peers))

    swaps = [
        remote(
            source,
            tables[2 * i + 1],
            swap_sems.at[0, i],
            swap_sems.at[1, i],
            {"ctx": spot * 2 + 1 - side, "tp": tp},
        )
        for i, source in enumerate((th_ref, tm_ref, tt_ref))
    ]
    attention_phase(
        tp_count,
        ctx_count,
        hidden_ref,
        norm_gain_ref,
        weights,
        loads[:3],
        swaps,
        attention,
        attention_sems,
    )
    reduce_phase(
        tp_count,
        norm_gain_ref.shape[1],
        attention[-1],
        weights[3],
        hidden_ref,
        head_gain_ref,
        proj,
        hidden_out_ref,
        own,
        reduce,
        reduce_sems,
        loads[3:7],
    )
    loss_phase(
        line,
        tp_count,
        own,
        targets_ref,
        clusters_ref,
        tables,
        losses_ref,
        loss,
        loss_sems,
        loads[7:],
        swaps,
    )


def body(
    hidden_in,
    norm_gain,
    w_query,
    w_key,
    w_value,
    w_out,
    head_gain,
    proj_head,
    proj_middle,
    proj_tail,
    table_head,
    table_middle,
    table_tail,
    clusters,
    targets,
):
    tp_count = lax.axis_size("tp")
    line = lax.axis_size("ctx") // 2
    chips = tp_count // 2
    tokens, width = hidden_in.shape
    model_width = width * tp_count
    rows = tokens // tp_count
    bands = proj_head.shape[1] + proj_middle.shape[1] + proj_tail.shape[1]
    goals = jnp.broadcast_to(targets[None], (8, tokens))
    dma = pltpu.SemaphoreType.DMA
    large = (w_query, w_key, w_value, w_out, proj_head, proj_middle, proj_tail)
    tables = (table_head, table_middle, table_tail)
    vmem = pl.BlockSpec(memory_space=pltpu.VMEM)
    hidden_out, losses = pl.pallas_call(
        functools.partial(layer_kernel, line, tp_count),
        out_shape=(
            jax.ShapeDtypeStruct((tokens, width), BF16),
            jax.ShapeDtypeStruct((1, tokens), F32),
        ),
        in_specs=[vmem] * 5 + [pl.BlockSpec(memory_space=pl.ANY)] * 10,
        out_specs=(vmem, vmem),
        scratch_shapes=[pltpu.VMEM(a.shape, BF16) for a in large]
        + [pltpu.VMEM(a.shape, BF16) for a in tables for _ in range(2)]
        + [
            pltpu.VMEM((2, tokens, model_width), BF16),
            pltpu.VMEM((tokens, model_width), BF16),
            pltpu.VMEM((tokens, width), BF16),
            pltpu.VMEM((2 * tokens, width), BF16),
            pltpu.VMEM((2 * tokens, width), BF16),
            pltpu.VMEM((tokens, width), F32),
            pltpu.VMEM((tokens, width), BF16),
            pltpu.VMEM((rows, bands), BF16),
        ]
        + [pltpu.VMEM((chips, tokens, width), BF16)] * 4
        + [pltpu.VMEM((tokens, bands), BF16)]
        + [pltpu.VMEM((chips, rows, bands), BF16)] * 3
        + [pltpu.VMEM((tokens, 128), F32), pltpu.VMEM((tp_count, rows, 128), F32)]
        + [
            pltpu.VMEM((line, tokens, bands), BF16),
            pltpu.VMEM((line, 8, tokens), jnp.int32),
            pltpu.VMEM((line, 8, tokens), F32),
            pltpu.VMEM((line * tp_count, 8, tokens), F32),
        ]
        + [dma((10,)), dma((2, 3))]
        + [dma((2,)), dma((2, 2, chips)), dma((2, 2, chips))]
        + [dma((2, chips))] * 4
        + [dma((2, tp_count))]
        + [
            dma((2, line + 1)),
            dma((2, line + 1)),
            dma((2, line, chips)),
            dma((2, line, chips)),
            dma((2, line)),
            dma((2, line, tp_count)),
        ],
        compiler_params=pltpu.CompilerParams(
            collective_id=0, has_side_effects=True, vmem_limit_bytes=62 * 1024 * 1024
        ),
    )(
        hidden_in,
        norm_gain[None],
        head_gain[None],
        clusters,
        goals,
        *large,
        *tables,
    )
    return (hidden_out, losses[0])


def solution(mesh):
    placed = (
        P("ctx", "tp"),
        P(),
        P(None, "tp"),
        P(None, "tp"),
        P(None, "tp"),
        P("tp", None),
        P(),
        P("tp", None),
        P("tp", None),
        P("tp", None),
        P(("tp", "ctx"), None),
        P(("tp", "ctx"), None),
        P(("tp", "ctx"), None),
        P(),
        P("ctx"),
    )
    return jax.shard_map(
        body, mesh=mesh, in_specs=placed, out_specs=(P("ctx", "tp"), P("ctx")), check_vma=False
    )
```

```python
import functools

import jax
import jax.numpy as jnp
from jax import lax
from jax.experimental import pallas as pl
from jax.experimental.pallas import tpu as pltpu
from jax.sharding import PartitionSpec as P

HD = 96
NEG_FILL = -1e30
EPS = 1e-06
F32 = jnp.float32
BF16 = jnp.bfloat16


def chunk_of(rows):
    best = rows
    if rows > 1024:
        for size in range(16, 1025, 16):
            if rows % size == 0:
                best = size
    return best


def band_stats(band, table_ref, goal):
    rows = table_ref.shape[0]
    chunk = chunk_of(rows)
    top = total = pick = None
    for start in range(0, rows, chunk):
        logits = lax.dot_general(
            table_ref[start : start + chunk, :],
            band,
            (((1,), (1,)), ((), ())),
            preferred_element_type=F32,
        )
        word = lax.broadcasted_iota(jnp.int32, logits.shape, 0)
        chosen = jnp.sum(jnp.where(word == goal - start, logits, 0.0), 0, keepdims=True)
        peak = jnp.max(logits, 0, keepdims=True)
        if top is None:
            top = peak
            total = jnp.sum(jnp.exp(logits - top), 0, keepdims=True)
            pick = chosen
        else:
            higher = jnp.maximum(top, peak)
            total = total * jnp.exp(top - higher) + jnp.sum(
                jnp.exp(logits - higher), 0, keepdims=True
            )
            top = higher
            pick = pick + chosen
    return top, total, pick


MESH = pl.DeviceIdType.MESH


def tp_device(rank):
    return {"ctx": lax.axis_index("ctx"), "tp": rank}


def remote(src, dst, send_sem, recv_sem, device):
    return pltpu.make_async_remote_copy(
        src_ref=src,
        dst_ref=dst,
        send_sem=send_sem,
        recv_sem=recv_sem,
        device_id=device,
        device_id_type=MESH,
    )


def reduce_phase(
    tp_count,
    model_width,
    context_ref,
    w_out_ref,
    hidden_ref,
    gain_ref,
    proj_refs,
    hidden_out_ref,
    own_ref,
    buffers,
    sems,
    loads,
    attend,
):
    a_send, a_recv, b_send, b_recv, part, c_recv, d_send, d_recv, sq_part, sq_recv = buffers
    a_sems, b_sems, c_sems, d_sems, sq_sems = sems
    proj_head_ref, proj_middle_ref, proj_tail_ref = proj_refs
    chips = tp_count // 2
    tp = lax.axis_index("tp")
    chip, core = tp // 2, tp % 2
    partner = tp_device(chip * 2 + 1 - core)
    width = hidden_ref.shape[1]
    rows = own_ref.shape[0]

    def columns(rank):
        return pl.ds(pl.multiple_of(rank * width, width), width)

    def tokens(rank):
        return pl.ds(pl.multiple_of(rank * rows, rows), rows)

    order = list(range(1, chips)) + [0]
    pending = []
    kept = []
    half_len = hidden_ref.shape[0] // 2

    def lines(half):
        return pl.ds(half * half_len, half_len)

    def core_copy(j, half):
        return remote(
            a_send.at[j, lines(half), :],
            a_recv.at[j, lines(half), :],
            a_sems.at[0, j, half],
            a_sems.at[1, j, half],
            partner,
        )

    def chip_copy(j, half):
        return remote(
            b_send.at[j, lines(half), :],
            b_recv.at[j, lines(half), :],
            b_sems.at[0, j, half],
            b_sems.at[1, j, half],
            tp_device(((chip + j) % chips) * 2 + core),
        )

    for half in range(2):
        attend(half)
        if half == 0:
            loads[0].wait()
        context = context_ref[lines(half), :]
        for j in order:
            there = (chip + j) % chips
            a_send[j, lines(half), :] = jnp.dot(
                context, w_out_ref[:, columns(there * 2 + 1 - core)], preferred_element_type=F32
            ).astype(BF16)
            copy = core_copy(j, half)
            copy.start()
            pending.append(copy)
            mine = jnp.dot(
                context, w_out_ref[:, columns(there * 2 + core)], preferred_element_type=F32
            )
            if j > 0:
                copy.wait_recv()
                b_send[j, lines(half), :] = (
                    mine + a_recv[j, lines(half), :].astype(F32)
                ).astype(BF16)
                copy = chip_copy(j, half)
                copy.start()
                pending.append(copy)
            else:
                kept.append(mine)
    for load in loads[1:]:
        load.wait()
    first = proj_head_ref.shape[1]
    second = first + proj_middle_ref.shape[1]
    for half in range(2):
        core_copy(0, half).wait_recv()
        acc = kept[half] + a_recv[0, lines(half), :].astype(F32)
        for j in range(1, chips):
            chip_copy(j, half).wait_recv()
            acc = acc + b_recv[j, lines(half), :].astype(F32)
        summed = hidden_ref[lines(half), :].astype(F32) + acc
        hidden_out_ref[lines(half), :] = summed.astype(BF16)
        squares = jnp.sum(summed * summed, 1, keepdims=True)
        sq_part[lines(half), :] = jnp.broadcast_to(squares, (half_len, sq_part.shape[1]))
        scaled = (summed * gain_ref[:, columns(tp)]).astype(BF16)
        part[lines(half), :first] = jnp.dot(
            scaled, proj_head_ref[...], preferred_element_type=F32
        ).astype(BF16)
        part[lines(half), first:second] = jnp.dot(
            scaled, proj_middle_ref[...], preferred_element_type=F32
        ).astype(BF16)
        part[lines(half), second:] = jnp.dot(
            scaled, proj_tail_ref[...], preferred_element_type=F32
        ).astype(BF16)
    for step in range(1, tp_count):
        there = (tp + step) % tp_count
        copy = remote(
            sq_part.at[tokens(there), :],
            sq_recv.at[step],
            sq_sems.at[0, step],
            sq_sems.at[1, step],
            tp_device(there),
        )
        copy.start()
        pending.append(copy)

    for j in order:
        there = (chip + j) % chips
        copy = remote(
            part.at[tokens(there * 2 + 1 - core), :],
            c_recv.at[j],
            c_sems.at[0, j],
            c_sems.at[1, j],
            partner,
        )
        copy.start()
        pending.append(copy)
    acc = None
    for j in order:
        there = (chip + j) % chips
        remote(
            part.at[tokens(there * 2 + 1 - core), :],
            c_recv.at[j],
            c_sems.at[0, j],
            c_sems.at[1, j],
            partner,
        ).wait_recv()
        mine = part[tokens(there * 2 + core), :].astype(F32) + c_recv[j].astype(F32)
        if j > 0:
            d_send[j] = mine.astype(BF16)
            copy = remote(
                d_send.at[j],
                d_recv.at[j],
                d_sems.at[0, j],
                d_sems.at[1, j],
                tp_device(there * 2 + core),
            )
            copy.start()
            pending.append(copy)
        else:
            acc = mine
    total_sq = sq_part[tokens(tp), :]
    for step in range(1, tp_count):
        remote(
            sq_part.at[tokens(tp), :],
            sq_recv.at[step],
            sq_sems.at[0, step],
            sq_sems.at[1, step],
            partner,
        ).wait_recv()
        total_sq = total_sq + sq_recv[step]
    row_scale = lax.rsqrt(total_sq[:, :1] / model_width + EPS)
    for j in range(1, chips):
        remote(d_send.at[j], d_recv.at[j], d_sems.at[0, j], d_sems.at[1, j], partner).wait_recv()
        acc = acc + d_recv[j].astype(F32)
    own_ref[...] = (acc * row_scale).astype(BF16)
    for copy in pending:
        copy.wait_send()


def combined(one, other):
    top = jnp.maximum(one[0], other[0])
    return (
        top,
        one[1] * jnp.exp(one[0] - top) + other[1] * jnp.exp(other[0] - top),
        one[2] + other[2],
    )


def loss_phase(
    line,
    tp_count,
    own_ref,
    targets_ref,
    clusters_ref,
    table_refs,
    losses_ref,
    buffers,
    sems,
    loads,
    swaps,
):
    head_ref, middle_ref = table_refs[0], table_refs[2]
    bands, goals, stat_send, stat_recv = buffers
    z_send, z_recv, y_sems, c_sems, g_sems, s_sems = sems
    chips = tp_count // 2
    tp = lax.axis_index("tp")
    ctx = lax.axis_index("ctx")
    chip, core = tp // 2, tp % 2
    spot, side = ctx // 2, ctx % 2
    rows = own_ref.shape[0]
    ctx_count = line * 2
    v0 = head_ref.shape[0] * tp_count * ctx_count
    v1 = middle_ref.shape[0] * tp_count * ctx_count

    def device(place, rank):
        return {"ctx": place * 2 + side, "tp": rank}

    def shard(source, rank):
        return bands.at[source, pl.ds(pl.multiple_of(rank * rows, rows), rows), :]

    def along(d, source, way):
        there = spot + 1 if way == 0 else spot - 1
        piece = shard(source, tp)
        return remote(
            piece, piece, z_send.at[way, d], z_recv.at[way, d + 1], device(there, tp)
        )

    def arrival(d, source, way):
        piece = shard(source, tp)
        return remote(piece, piece, z_send.at[way, d], z_recv.at[way, d], device(spot, tp))

    def sideways(source, j):
        piece = shard(source, tp)
        there = ((chip + j) % chips) * 2 + core
        return remote(
            piece, piece, y_sems.at[0, source, j], y_sems.at[1, source, j], device(spot, there)
        )

    def from_side(source, j):
        piece = shard(source, ((chip - j + chips) % chips) * 2 + core)
        return remote(
            piece, piece, y_sems.at[0, source, j], y_sems.at[1, source, j], device(spot, tp)
        )

    def across(source, j, owner_core):
        piece = shard(source, ((chip - j + chips) % chips) * 2 + owner_core)
        return remote(
            piece,
            piece,
            c_sems.at[0, source, j],
            c_sems.at[1, source, j],
            device(spot, chip * 2 + 1 - core),
        )

    def spread(source):
        for j in range(1, chips):
            sideways(source, j).start()
        across(source, 0, core).start()

    def goal_copy(k):
        return remote(
            goals.at[spot],
            goals.at[spot],
            g_sems.at[0, k],
            g_sems.at[1, k],
            device((spot + k) % line, tp),
        )

    def stat_copy(source, t):
        return remote(
            stat_send.at[source],
            stat_recv.at[spot * tp_count + tp],
            s_sems.at[0, source, t],
            s_sems.at[1, spot, t],
            device(source, (tp + t) % tp_count),
        )

    bands[spot, pl.ds(pl.multiple_of(tp * rows, rows), rows), :] = own_ref[...]
    goals[spot] = jnp.broadcast_to(targets_ref[...], goals.shape[1:])

    @pl.when(spot + 1 < line)
    def _():
        along(0, spot, 0).start()

    @pl.when(spot > 0)
    def _():
        along(0, spot, 1).start()

    spread(spot)
    for k in range(1, line):
        goal_copy(k).start()
    place_own = tp * ctx_count + ctx
    place_pair = tp * ctx_count + spot * 2 + 1 - side
    first = head_ref.shape[1]
    second = first + middle_ref.shape[1]

    def finish(source):
        for j in range(1, chips):
            from_side(source, j).wait_recv()
            across(source, j, core).start()
        for j in range(chips):
            across(source, j, 1 - core).wait_recv()
        goal = goals[source][0:1, :]

        limits = (0, first, second, bands.shape[2])
        bases = (0, v0, v0 + v1)

        def found_in(i, table, place):
            return band_stats(
                bands[source, :, limits[i] : limits[i + 1]],
                table,
                goal - bases[i] - place * table.shape[0],
            )

        own_found = [found_in(i, table_refs[2 * i], place_own) for i in range(3)]

        @pl.when(source == spot)
        def _():
            for swap in swaps:
                swap.wait()

        one, two, three = [
            combined(own_found[i], found_in(i, table_refs[2 * i + 1], place_pair))
            for i in range(3)
        ]
        found = (one[0], one[1], two[0], two[1], three[0], three[1], one[2] + two[2] + three[2])
        for i, value in enumerate(found):
            stat_send[source, i : i + 1, :] = value
        stat_send[source, 7:8, :] = jnp.zeros_like(one[0])
        for t in range(1, tp_count):
            stat_copy(source, t).start()

        @pl.when(source != spot)
        def _():
            stat_copy(source, 0).start()

    def pass_on(d):
        @pl.when((d + 1 < line) & (spot - d - 1 >= 0))
        def _():
            source = spot - d - 1
            arrival(d + 1, source, 0).wait_recv()

            @pl.when(spot + 1 < line)
            def _():
                along(d + 1, source, 0).start()

            spread(source)

        @pl.when((d + 1 < line) & (spot + d + 1 < line))
        def _():
            source = spot + d + 1
            arrival(d + 1, source, 1).wait_recv()

            @pl.when(spot > 0)
            def _():
                along(d + 1, source, 1).start()

            spread(source)

    def step(d, carry):
        @pl.when(d > 0)
        def _():
            pass_on(d)

        @pl.when(spot - d >= 0)
        def _():
            finish(spot - d)

        @pl.when((d > 0) & (spot + d < line))
        def _():
            finish(spot + d)

        return carry

    pass_on(0)
    for k in range(1, line):
        place = (spot - k + line) % line
        remote(
            goals.at[place], goals.at[place], g_sems.at[0, k], g_sems.at[1, k], device(spot, tp)
        ).wait_recv()

    for load in loads:
        load.wait()
    lax.fori_loop(0, line, step, 0)

    stat_recv[spot * tp_count + tp] = stat_send[spot]
    clusters = lax.dot_general(
        clusters_ref[...],
        bands[spot, :, :first],
        (((1,), (1,)), ((), ())),
        preferred_element_type=F32,
    )
    for k in range(line):
        place = (spot + k) % line
        for t in range(tp_count):
            if k or t:
                slot = stat_recv.at[place * tp_count + (tp - t + tp_count) % tp_count]
                remote(
                    slot, slot, s_sems.at[0, place, t], s_sems.at[1, place, t], device(spot, tp)
                ).wait_recv()

    def total_of(i):
        tops = stat_recv[:, i, :]
        top = jnp.max(tops, 0, keepdims=True)
        return top + jnp.log(
            jnp.sum(stat_recv[:, i + 1, :] * jnp.exp(tops - top), 0, keepdims=True)
        )

    words = total_of(0)
    middle_total = total_of(2)
    tail_total = total_of(4)
    pick = jnp.sum(stat_recv[:, 6, :], 0, keepdims=True)
    first_cluster, second_cluster = clusters[0:1, :], clusters[1:2, :]
    top = jnp.maximum(words, jnp.maximum(first_cluster, second_cluster))
    head_total = top + jnp.log(
        jnp.exp(words - top) + jnp.exp(first_cluster - top) + jnp.exp(second_cluster - top)
    )
    goal = targets_ref[0:1, :]
    extra = jnp.where(
        goal < v0,
        0.0,
        jnp.where(goal < v0 + v1, middle_total - first_cluster, tail_total - second_cluster),
    )
    losses_ref[...] = head_total + extra - pick

    for k in range(1, line):
        goal_copy(k).wait_send()

    def settle(source, carry):
        for j in range(1, chips):
            sideways(source, j).wait_send()
        for j in range(chips):
            across(source, j, core).wait_send()
        for t in range(1, tp_count):
            stat_copy(source, t).wait_send()

        @pl.when(source != spot)
        def _():
            stat_copy(source, 0).wait_send()

        @pl.when((spot + 1 < line) & (spot - source >= 0))
        def _():
            along(source, spot - source, 0).wait_send()

        @pl.when((spot > 0) & (spot + source < line))
        def _():
            along(source, spot + source, 1).wait_send()

        return carry

    lax.fori_loop(0, line, settle, 0)


def attention_phase(
    tp_count,
    ctx_count,
    hidden_ref,
    gain_ref,
    weights,
    loads,
    swaps,
    buffers,
    sems,
):
    rows, normed, queries, keys, values, acc, context_ref = buffers
    p_sems, y_sems, c_sems = sems
    chips = tp_count // 2
    tp = lax.axis_index("tp")
    ctx = lax.axis_index("ctx")
    chip, core = tp // 2, tp % 2
    seg_len, width = hidden_ref.shape
    group = 4 * HD

    def shard(part, rank):
        return rows.at[part, :, pl.ds(pl.multiple_of(rank * width, width), width)]

    def sideways(part, j):
        piece = shard(part, tp)
        there = ((chip + j) % chips) * 2 + core
        return remote(
            piece, piece, y_sems.at[0, part, j], y_sems.at[1, part, j], tp_device(there)
        )

    def from_side(part, j):
        piece = shard(part, ((chip - j + chips) % chips) * 2 + core)
        return remote(piece, piece, y_sems.at[0, part, j], y_sems.at[1, part, j], tp_device(tp))

    def across(part, j, owner_core):
        piece = shard(part, ((chip - j + chips) % chips) * 2 + owner_core)
        return remote(
            piece,
            piece,
            c_sems.at[0, part, j],
            c_sems.at[1, part, j],
            tp_device(chip * 2 + 1 - core),
        )

    def spread(part):
        for j in range(1, chips):
            sideways(part, j).start()
        across(part, 0, core).start()

    def relay(part):
        for j in range(1, chips):
            from_side(part, j).wait_recv()
            across(part, j, core).start()

    def normalise(part):
        for j in range(chips):
            across(part, j, 1 - core).wait_recv()
        wide = rows[part].astype(F32)
        mean_sq = jnp.mean(wide * wide, axis=1, keepdims=True)
        normed[...] = (wide * lax.rsqrt(mean_sq + EPS) * gain_ref[...]).astype(BF16)

    def project(weight, out, start):
        def tile(i, carry):
            cut = pl.ds(pl.multiple_of(i * group, group), group)
            out[start : start + seg_len, cut] = jnp.dot(
                normed[...], weight[:, cut], preferred_element_type=F32
            ).astype(BF16)
            return carry

        lax.fori_loop(0, width // group, tile, 0)

    rows[1, :, pl.ds(pl.multiple_of(tp * width, width), width)] = hidden_ref[...]
    forward = remote(
        shard(1, tp),
        shard(0, tp),
        p_sems.at[0],
        p_sems.at[1],
        {"ctx": (ctx + 1) % ctx_count, "tp": tp},
    )
    forward.start()
    spread(1)
    relay(1)
    forward.wait_recv()
    spread(0)
    for swap in swaps:
        swap.start()
    normalise(1)
    for load in loads:
        load.wait()
    project(weights[0], queries, 0)
    project(weights[1], keys, seg_len)
    project(weights[2], values, seg_len)
    relay(0)
    normalise(0)
    project(weights[1], keys, 0)
    project(weights[2], values, 0)

    half_len = seg_len // 2
    acc[...] = jnp.zeros_like(acc)

    def attend(half):
        start = half * half_len
        span = seg_len + start + half_len

        def heads(i, carry):
            for h in range(4):
                low = h * HD // 128 * 128
                high = -(-(h + 1) * HD // 128) * 128
                cut = pl.ds(pl.multiple_of(i * group + low, 128), high - low)
                lane = lax.broadcasted_iota(jnp.int32, (half_len, high - low), 1) + low
                inside = (lane >= h * HD) & (lane < (h + 1) * HD)
                query = jnp.where(
                    inside, queries[start : start + half_len, cut].astype(F32), 0.0
                ).astype(BF16)
                scores = lax.dot_general(
                    query,
                    keys[:span, cut],
                    (((1,), (1,)), ((), ())),
                    preferred_element_type=F32,
                ) * HD ** (-0.5)
                row_pos = lax.broadcasted_iota(jnp.int32, scores.shape, 0) + start
                col_pos = lax.broadcasted_iota(jnp.int32, scores.shape, 1)
                first = jnp.where(ctx > 0, 0, seg_len)
                allowed = (col_pos >= first) & (col_pos - seg_len <= row_pos)
                scores = jnp.where(allowed, scores, NEG_FILL)
                raised = jnp.exp(scores - jnp.max(scores, axis=1, keepdims=True))
                shares = (raised / jnp.sum(raised, axis=1, keepdims=True)).astype(BF16)
                mixed = jnp.dot(shares, values[:span, cut], preferred_element_type=F32)
                acc[start : start + half_len, cut] = jnp.where(
                    inside, mixed, acc[start : start + half_len, cut]
                )
            return carry

        lax.fori_loop(0, width // group, heads, 0)
        context_ref[start : start + half_len, :] = acc[start : start + half_len, :].astype(BF16)

    def settle():
        forward.wait_send()
        for part in range(2):
            for j in range(1, chips):
                sideways(part, j).wait_send()
            for j in range(chips):
                across(part, j, core).wait_send()

    return attend, settle


def layer_kernel(line, tp_count, *refs):
    (
        hidden_ref,
        norm_gain_ref,
        head_gain_ref,
        clusters_ref,
        targets_ref,
        wq_ref,
        wk_ref,
        wv_ref,
        wo_ref,
        ph_ref,
        pm_ref,
        pt_ref,
        th_ref,
        tm_ref,
        tt_ref,
        hidden_out_ref,
        losses_ref,
    ) = refs[:17]
    held = refs[17:30]
    weights, proj = held[0:4], held[4:7]
    tables = held[7:13]
    attention = refs[30:37]
    own = refs[37]
    reduce = refs[38:48]
    loss = refs[48:52]
    load_sems, swap_sems = refs[52:54]
    attention_sems = refs[54:57]
    reduce_sems = refs[57:62]
    loss_sems = refs[62:68]
    ctx_count = line * 2
    tp = lax.axis_index("tp")
    ctx = lax.axis_index("ctx")
    spot, side = ctx // 2, ctx % 2

    sources = (wq_ref, wk_ref, wv_ref, wo_ref, ph_ref, pm_ref, pt_ref, th_ref, tm_ref, tt_ref)
    targets = weights + proj + tables[0::2]
    loads = [
        pltpu.make_async_copy(source, target, load_sems.at[i])
        for i, (source, target) in enumerate(zip(sources, targets))
    ]
    for load in loads:
        load.start()

    barrier = pltpu.get_barrier_semaphore()
    peers = [
        {"ctx": ((spot + k) % line) * 2 + side, "tp": (tp + t) % tp_count}
        for k in range(line)
        for t in range(tp_count)
        if k or t
    ]
    peers += [
        {"ctx": (ctx + 1) % ctx_count, "tp": tp},
        {"ctx": (ctx + ctx_count - 1) % ctx_count, "tp": tp},
    ]
    for peer in peers:
        pl.semaphore_signal(barrier, inc=1, device_id=peer, device_id_type=MESH)
    pl.semaphore_wait(barrier, len(peers))

    swaps = [
        remote(
            source,
            tables[2 * i + 1],
            swap_sems.at[0, i],
            swap_sems.at[1, i],
            {"ctx": spot * 2 + 1 - side, "tp": tp},
        )
        for i, source in enumerate((th_ref, tm_ref, tt_ref))
    ]
    attend, settle = attention_phase(
        tp_count,
        ctx_count,
        hidden_ref,
        norm_gain_ref,
        weights,
        loads[:3],
        swaps,
        attention,
        attention_sems,
    )
    reduce_phase(
        tp_count,
        norm_gain_ref.shape[1],
        attention[-1],
        weights[3],
        hidden_ref,
        head_gain_ref,
        proj,
        hidden_out_ref,
        own,
        reduce,
        reduce_sems,
        loads[3:7],
        attend,
    )
    loss_phase(
        line,
        tp_count,
        own,
        targets_ref,
        clusters_ref,
        tables,
        losses_ref,
        loss,
        loss_sems,
        loads[7:],
        swaps,
    )
    settle()


def body(
    hidden_in,
    norm_gain,
    w_query,
    w_key,
    w_value,
    w_out,
    head_gain,
    proj_head,
    proj_middle,
    proj_tail,
    table_head,
    table_middle,
    table_tail,
    clusters,
    targets,
):
    tp_count = lax.axis_size("tp")
    line = lax.axis_size("ctx") // 2
    chips = tp_count // 2
    tokens, width = hidden_in.shape
    model_width = width * tp_count
    rows = tokens // tp_count
    bands = proj_head.shape[1] + proj_middle.shape[1] + proj_tail.shape[1]
    dma = pltpu.SemaphoreType.DMA
    large = (w_query, w_key, w_value, w_out, proj_head, proj_middle, proj_tail)
    tables = (table_head, table_middle, table_tail)
    vmem = pl.BlockSpec(memory_space=pltpu.VMEM)
    hidden_out, losses = pl.pallas_call(
        functools.partial(layer_kernel, line, tp_count),
        out_shape=(
            jax.ShapeDtypeStruct((tokens, width), BF16),
            jax.ShapeDtypeStruct((1, tokens), F32),
        ),
        in_specs=[vmem] * 5 + [pl.BlockSpec(memory_space=pl.ANY)] * 10,
        out_specs=(vmem, vmem),
        scratch_shapes=[pltpu.VMEM(a.shape, BF16) for a in large]
        + [pltpu.VMEM(a.shape, BF16) for a in tables for _ in range(2)]
        + [
            pltpu.VMEM((2, tokens, model_width), BF16),
            pltpu.VMEM((tokens, model_width), BF16),
            pltpu.VMEM((tokens, width), BF16),
            pltpu.VMEM((2 * tokens, width), BF16),
            pltpu.VMEM((2 * tokens, width), BF16),
            pltpu.VMEM((tokens, width), F32),
            pltpu.VMEM((tokens, width), BF16),
            pltpu.VMEM((rows, bands), BF16),
        ]
        + [pltpu.VMEM((chips, tokens, width), BF16)] * 4
        + [pltpu.VMEM((tokens, bands), BF16)]
        + [pltpu.VMEM((chips, rows, bands), BF16)] * 3
        + [pltpu.VMEM((tokens, 128), F32), pltpu.VMEM((tp_count, rows, 128), F32)]
        + [
            pltpu.VMEM((line, tokens, bands), BF16),
            pltpu.VMEM((line, 8, tokens), jnp.int32),
            pltpu.VMEM((line, 8, tokens), F32),
            pltpu.VMEM((line * tp_count, 8, tokens), F32),
        ]
        + [dma((10,)), dma((2, 3))]
        + [dma((2,)), dma((2, 2, chips)), dma((2, 2, chips))]
        + [dma((2, chips, 2))] * 2
        + [dma((2, chips))] * 2
        + [dma((2, tp_count))]
        + [
            dma((2, line + 1)),
            dma((2, line + 1)),
            dma((2, line, chips)),
            dma((2, line, chips)),
            dma((2, line)),
            dma((2, line, tp_count)),
        ],
        compiler_params=pltpu.CompilerParams(
            collective_id=0, has_side_effects=True, vmem_limit_bytes=62 * 1024 * 1024
        ),
    )(
        hidden_in,
        norm_gain[None],
        head_gain[None],
        clusters,
        targets[None],
        *large,
        *tables,
    )
    return (hidden_out, losses[0])


def solution(mesh):
    placed = (
        P("ctx", "tp"),
        P(),
        P(None, "tp"),
        P(None, "tp"),
        P(None, "tp"),
        P("tp", None),
        P(),
        P("tp", None),
        P("tp", None),
        P("tp", None),
        P(("tp", "ctx"), None),
        P(("tp", "ctx"), None),
        P(("tp", "ctx"), None),
        P(),
        P("ctx"),
    )
    return jax.shard_map(
        body, mesh=mesh, in_specs=placed, out_specs=(P("ctx", "tp"), P("ctx")), check_vma=False
    )
```
